32 devices in a mesh: dp: 4 (over z), cp: 8 (over y, x, core).
Axes of the slice: x: 2, y: 2, z: 4, core: 2. Of those that a mesh axis runs over, the one named last changes fastest.
Arguments:
- table_rows: bfloat16 [65536, 1024], P(('dp', 'cp')), may hold values from -6 to 6
- row_scales: float32 [65536], P(('dp', 'cp')), may hold values from 0.25 to 4
- owners: int32 [4096, 1], P(('dp', 'cp')), may hold values from 0 to 31; in each aligned block of 128 rows (0 to 127, 128 to 255, ...) at most 8 rows name the same one
- shard_rows: int32 [4096], P(('dp', 'cp')), may hold values from 0 to 2047
- history_lengths: int32 [4, 3], P('dp'), may hold values from 1 to 512, 1024 in all within a row
- input_weight: bfloat16 [1024, 4096], replicated, may hold values from -0.1875 to 0.1875
- output_weight: bfloat16 [1024, 1024], replicated, may hold values from -0.1875 to 0.1875
- cotangent: bfloat16 [4096, 1024], P(('dp', 'cp')), may hold values from -6 to 6
Outputs:
- layer_out: bfloat16 [4096, 1024], P(('dp', 'cp'))
- table_grad: float32 [65536, 1024], P(('dp', 'cp'))
The draws below stay inside these ranges and needn't reach their ends.
Inputs may be any that keep to these rules, and one draw needn't show every extreme that they name: `owners`: among the events of one device no shard is named more than 8 times, and some device names one shard exactly 8 times. `history_lengths`: the 3 lengths of a cycle group sum to 1024; the longest is exactly 512.
All inputs are finite; a program needn't handle non-finite values.
Results may differ from the reference program's by a relative error of at most 0.0043.
Values may be sent and summed in bfloat16 or wider, within the bound.
A program may use at most 128 MiB of HBM per device.

```python
import math
import jax
import jax.numpy as jnp
import numpy as np
from jax import lax

D = 1024
HEADS = 8
HDIM = 128
TAB_DEV = 2048
NDOC = 3
ROWS = 128
SHARDS = 32
GROUPS = 4
CAP = 8
CYCLE = 1024
LMAX = 512
TOKENS = 4096
VOCAB = 65536
N_CP = 8


def with_ends(entries, rng, least, high):
    longest = entries.shape.index(max(entries.shape))
    spots = []
    for shift in (0, 1):
        where = [jax.random.randint(jax.random.fold_in(rng, axis), (), 0, length) for axis, length in enumerate(entries.shape)]
        where[longest] = (where[longest] + shift) % entries.shape[longest]
        spots.append(tuple(where))
    return entries.at[spots[0]].set(least).at[spots[1]].set(high)


def block_levels(rng, extent, pieces, low, largest):
    def one(axis_at, parts):
        draws = jax.random.uniform(jax.random.fold_in(jax.random.fold_in(rng, 6), axis_at), (parts,), jnp.float32, low / len(pieces), largest / len(pieces))
        return jnp.repeat(jnp.exp(draws), extent[axis_at] // parts).reshape((-1,) + (1,) * (len(extent) - axis_at - 1))

    gain = one(*pieces[0])
    for cut in pieces[1:]:
        gain = gain * one(*cut)
    return gain


def split_up(amount, total, reach, slope):
    portions = [(1 << 20) // math.isqrt(grade ** slope) + 1 for grade in range(2, amount + 1)]
    surplus, holding = total - reach - (amount - 1), [1] * (amount - 1)
    while surplus > 0:
        movable = [i for i in range(amount - 1) if holding[i] < reach]
        pool, left = sum([portions[i] for i in movable]), surplus
        for i in movable:
            addition = min(reach - holding[i], max(1, left * portions[i] // pool), surplus)
            holding[i] = holding[i] + addition
            surplus = surplus - addition
    return np.array([reach] + holding)


def ragged(rng, count, total, most, lean):
    if count == 2:
        one = jax.random.randint(rng, (), max(1, total - most), min(most, total - 1) + 1)
        return jnp.stack([one, total - one])
    tallies = jnp.asarray(split_up(count, total, most, lean), jnp.int32)
    couples = (count - 1) // 2
    donor, receiver = tallies[1:1 + 2 * couples:2], tallies[2:2 + 2 * couples:2]
    margin = jnp.minimum(donor - 1, most - receiver)
    moved = jax.random.randint(jax.random.fold_in(rng, 1), (couples,), 0, 1 << 20) % (margin + 1)
    tallies = tallies.at[1:1 + 2 * couples:2].set(donor - moved).at[2:2 + 2 * couples:2].set(receiver + moved)
    return tallies[jax.random.permutation(jax.random.fold_in(rng, 2), count)]


def routed_block(key, own, number, rows, count, top, most, lean):
    ranking = jax.random.permutation(key, count)
    crowded, usual = shares(count, rows * top, most, lean, True), shares(count, rows * top, most, lean, False)
    places = jnp.arange(count)

    def named(sizes, rotation):
        used = int((sizes > 0).sum())
        fixed = max(1, used // 4)
        moved = fixed + (places - fixed + rotation * (used - fixed)) % max(1, count - fixed)
        return jnp.zeros((count,), jnp.int32).at[ranking[jnp.where(places < fixed, places, moved)]].set(jnp.asarray(sizes, jnp.int32))

    sizes = jnp.where(number % 4 == 0, named(crowded, number // 4), named(usual, number - number // 4 - 1))
    mixed = jax.random.permutation(jax.random.fold_in(own, 3), count)
    source_of, sink = mixed[0:count // 2 * 2:2], mixed[1:count // 2 * 2:2]
    room = jnp.minimum(sizes[source_of] - 1, most - sizes[sink]) // 2
    room = jnp.where((source_of == ranking[0]) | (sink == ranking[0]) | (sizes[sink] == 0), 0, jnp.maximum(room, 0))
    moved = jax.random.randint(jax.random.fold_in(own, 4), (count // 2,), 0, 1 << 20) % (room + 1)
    sizes = sizes.at[source_of].add(-moved).at[sink].add(moved)
    items = jnp.searchsorted(jnp.cumsum(sizes), jnp.arange(rows * top), side="right").astype(jnp.int32)
    table = items.reshape(top, rows).T
    table = table[jax.random.permutation(jax.random.fold_in(own, 1), rows)]
    rotation = jax.random.randint(jax.random.fold_in(own, 2), (rows, 1), 0, top)
    return jnp.take_along_axis(table, (jnp.arange(top)[None, :] + rotation) % top, axis=1)


def shares(count, total, reach, slope, full):
    weights = [(1 << 20) // math.isqrt(grade ** slope) + 1 for grade in range(1, count + 1)]
    largest = reach if full else min(reach, max(-(-total // count), total * weights[0] // sum(weights)))
    least = 1 if total - largest >= count - 1 else 0
    given, surplus = [largest] + [least] * (count - 1), total - largest - least * (count - 1)
    while surplus > 0:
        free = [i for i in range(1, count) if given[i] < largest] or [i for i in range(1, count) if given[i] < reach]
        whole, remaining = sum([weights[i] for i in free]), surplus
        for i in free:
            more = min(reach - given[i], max(1, remaining * weights[i] // whole), surplus)
            given[i] = given[i] + more
            surplus = surplus - more
    return np.array(given)


def centred(stream_key, dims, deviation, reach, cuts=(), held_as=jnp.bfloat16):
    result = deviation * jax.random.normal(stream_key, dims, jnp.float32)
    if cuts:
        result = result * block_levels(stream_key, dims, cuts, -0.22, 0.18)
    return jnp.clip(result, -reach, reach).astype(held_as)


def setup_inputs(seed: int = 0) -> dict:
    splits = jax.random.split(jax.random.key(seed), 9)
    table_rows = centred(splits[0], (VOCAB, D), 1.0, 6.0, ((0, 32),))
    row_scales = jnp.clip(jnp.exp(math.log(4.0) - 2.7725887 * jax.random.uniform(splits[1], (VOCAB,), jnp.float32) ** block_levels(splits[1], (VOCAB,), ((0, 32),), -0.2, 0.2)), 0.25, 4.0)
    owners_keys = jax.random.split(jax.random.fold_in(splits[2], 1), TOKENS // ROWS)
    owners_turns = jax.random.permutation(jax.random.fold_in(splits[2], 3), TOKENS // ROWS)
    owners = jax.vmap(lambda own, number: routed_block(jax.random.fold_in(splits[2], 2), own, number, ROWS, SHARDS, 1, CAP, 2))(owners_keys, owners_turns).reshape((TOKENS, 1))
    shard_rows = with_ends(jax.random.randint(splits[3], (TOKENS,), 0, TAB_DEV), jax.random.fold_in(splits[3], 1), 0, TAB_DEV - 1).astype(jnp.int32)
    history_lengths = jax.vmap(lambda own: ragged(own, NDOC, CYCLE, LMAX, 2))(jax.random.split(splits[4], GROUPS)).reshape((GROUPS, NDOC)).astype(jnp.int32)
    input_weight = centred(splits[5], (D, 4 * D), D ** -0.5, 0.1875)
    output_weight = centred(splits[6], (D, D), D ** -0.5, 0.1875)
    cotangent = centred(splits[7], (TOKENS, D), 1.0, 6.0, ((0, 32),))
    return dict(table_rows=table_rows, row_scales=row_scales, owners=owners, shard_rows=shard_rows, history_lengths=history_lengths, input_weight=input_weight, output_weight=output_weight, cotangent=cotangent)


EPSILON = 1e-05

def doc_bounds(lengths, positions):
    lengths = lengths.astype(jnp.int32)
    ends_at = jnp.cumsum(lengths).astype(jnp.int32)
    begins_at = ends_at - lengths
    inside = (positions[:, None] >= begins_at[None, :]) & (positions[:, None] < ends_at[None, :])
    doc_first = lax.optimization_barrier(jnp.sum(jnp.where(inside, begins_at[None, :], 0), axis=1)).astype(jnp.int32)
    doc_length = lax.optimization_barrier(jnp.sum(jnp.where(inside, lengths[None, :], 0), axis=1)).astype(jnp.float32)
    return (doc_first, doc_length)

def normalize(values):
    center = lax.optimization_barrier(jnp.mean(values, axis=-1, keepdims=True))
    shifted = values - center
    inv_spread = lax.rsqrt(lax.optimization_barrier(jnp.mean(shifted * shifted, axis=-1, keepdims=True)) + EPSILON)
    return (shifted * inv_spread, inv_spread)

def normalize_back(grad_in, normed, inv_spread):
    return inv_spread * (grad_in - lax.optimization_barrier(jnp.mean(grad_in, axis=-1, keepdims=True)) - normed * lax.optimization_barrier(jnp.mean(grad_in * normed, axis=-1, keepdims=True)))

def score_block(queries, key_block, query_pos, query_first, key_pos):
    scaling = queries.shape[-1] ** (-0.5)
    scores = jnp.einsum('qhe,khe->hqk', queries.astype(jnp.float32), key_block.astype(jnp.float32)) * scaling
    allowed = (key_pos[None, :] >= query_first[:, None]) & (key_pos[None, :] <= query_pos[:, None])
    return (scores, allowed[None])

def forward_part(queries, key_block, value_block, query_pos, query_first, query_length, key_pos):
    scores, allowed = score_block(queries, key_block, query_pos, query_first, key_pos)
    weights = jnp.where(allowed, scores * jax.nn.sigmoid(scores) / query_length[None, :, None], 0.0).astype(jnp.bfloat16)
    return jnp.einsum('hqk,khe->qhe', weights.astype(jnp.float32), value_block.astype(jnp.float32))

def backward_part(queries, key_block, value_block, grad_out, query_pos, query_first, query_length, key_pos):
    scores, allowed = score_block(queries, key_block, query_pos, query_first, key_pos)
    sigmoid_part = jax.nn.sigmoid(scores)
    weights = jnp.where(allowed, scores * sigmoid_part / query_length[None, :, None], 0.0).astype(jnp.bfloat16)
    grad_weights = jnp.einsum('qhe,khe->hqk', grad_out.astype(jnp.float32), value_block.astype(jnp.float32))
    silu_slope = sigmoid_part * (1.0 + scores * (1.0 - sigmoid_part))
    scaling = queries.shape[-1] ** (-0.5)
    grad_scores = jnp.where(allowed, grad_weights * silu_slope / query_length[None, :, None] * scaling, 0.0).astype(jnp.bfloat16)
    grad_query = jnp.einsum('hqk,khe->qhe', grad_scores.astype(jnp.float32), key_block.astype(jnp.float32))
    grad_key = jnp.einsum('hqk,qhe->khe', grad_scores.astype(jnp.float32), queries.astype(jnp.float32))
    grad_value = jnp.einsum('hqk,qhe->khe', weights.astype(jnp.float32), grad_out.astype(jnp.float32))
    return (grad_query, grad_key, grad_value)

def reference(table_rows, row_scales, owners, shard_rows, history_lengths, input_weight, output_weight, cotangent):
    item_ids = (owners[:, 0] * TAB_DEV + shard_rows).astype(jnp.int32)
    embedded = table_rows[item_ids].astype(jnp.float32) * row_scales[item_ids][:, None]

    def one_group(packed):
        group_embed, group_grad, lengths = packed
        positions = jnp.arange(CYCLE, dtype=jnp.int32)
        query_first, query_length = doc_bounds(lengths, positions)
        normed, inv_embed = normalize(group_embed)
        projected = jnp.dot(normed.astype(jnp.bfloat16), input_weight, preferred_element_type=jnp.float32)
        activated = (projected * jax.nn.sigmoid(projected)).astype(jnp.bfloat16)
        gate_rows = activated[:, :D]
        value_heads = activated[:, D:2 * D].reshape(CYCLE, HEADS, HDIM)
        query_heads = activated[:, 2 * D:3 * D].reshape(CYCLE, HEADS, HDIM)
        key_heads = activated[:, 3 * D:].reshape(CYCLE, HEADS, HDIM)

        def shard_slices(shard):
            block_start = (shard * ROWS).astype(jnp.int32)
            return (lax.dynamic_slice_in_dim(query_heads, block_start, ROWS, 0), lax.dynamic_slice_in_dim(positions, block_start, ROWS, 0), lax.dynamic_slice_in_dim(query_first, block_start, ROWS, 0), lax.dynamic_slice_in_dim(query_length, block_start, ROWS, 0), block_start)

        def shard_forward(shard):
            queries, query_pos, first_part, length_part, block_start = shard_slices(shard)
            return forward_part(queries, key_heads, value_heads, query_pos, first_part, length_part, positions)
        shards = jnp.arange(N_CP, dtype=jnp.int32)
        attention = lax.map(shard_forward, shards).reshape(CYCLE, D)
        attn_norm, inv_attn = normalize(attention)
        mixed = attn_norm * gate_rows.astype(jnp.float32)
        output = group_embed + jnp.dot(mixed.astype(jnp.bfloat16), output_weight, preferred_element_type=jnp.float32)
        layer_part = output.astype(jnp.bfloat16)
        grad_mixed = jnp.dot(group_grad, output_weight.T, preferred_element_type=jnp.float32)
        grad_gate = grad_mixed * attn_norm
        grad_attn = normalize_back(grad_mixed * gate_rows.astype(jnp.float32), attn_norm, inv_attn).astype(jnp.bfloat16)
        grad_heads = grad_attn.reshape(CYCLE, HEADS, HDIM)

        def shard_backward(running, shard):
            queries, query_pos, first_part, length_part, block_start = shard_slices(shard)
            grad_piece = lax.dynamic_slice_in_dim(grad_heads, block_start, ROWS, 0)
            grad_query, grad_key, grad_value = backward_part(queries, key_heads, value_heads, grad_piece, query_pos, first_part, length_part, positions)
            return ((running[0] + grad_key, running[1] + grad_value), grad_query)
        zeros_all = jnp.zeros((CYCLE, HEADS, HDIM), jnp.float32)
        (grad_key, grad_value), grad_query = lax.scan(shard_backward, (zeros_all, zeros_all), shards)
        grad_act = jnp.concatenate([grad_gate, grad_value.reshape(CYCLE, D), grad_query.reshape(CYCLE, D), grad_key.reshape(CYCLE, D)], axis=1)
        sigmoid_part = jax.nn.sigmoid(projected)
        grad_proj = (grad_act * sigmoid_part * (1.0 + projected * (1.0 - sigmoid_part))).astype(jnp.bfloat16)
        grad_norm = jnp.dot(grad_proj, input_weight.T, preferred_element_type=jnp.float32)
        grad_embed = group_grad.astype(jnp.float32) + normalize_back(grad_norm, normed, inv_embed)
        return (layer_part, grad_embed)
    layer_out, grad_embed = lax.map(one_group, (embedded.reshape(GROUPS, CYCLE, D), cotangent.reshape(GROUPS, CYCLE, D), history_lengths))
    layer_out = layer_out.reshape(TOKENS, D)
    grad_embed = grad_embed.reshape(TOKENS, D)
    table_grad = row_scales[:, None] * jax.ops.segment_sum(grad_embed, item_ids, num_segments=VOCAB)
    return (layer_out, table_grad)
```

```python
import functools

import jax
import jax.numpy as jnp
from jax import lax
from jax.experimental import pallas as pl
from jax.experimental.pallas import tpu as pltpu
from jax.sharding import PartitionSpec as P

HEADS = 8
EPSILON = 1e-05
LANES = 128
MESH = pl.DeviceIdType.MESH
EXACT = lax.Precision.HIGHEST
F32 = jnp.float32
BF16 = jnp.bfloat16
VMEM_LIMIT = 60 * 1024 * 1024


def iota(shape, axis):
    return lax.broadcasted_iota(jnp.int32, shape, axis)


def dot_f32(a, b):
    return jnp.dot(a, b, precision=EXACT, preferred_element_type=F32)


def dot(a, b):
    return jnp.dot(a, b, preferred_element_type=F32)


def dot_nt(a, b):
    return lax.dot_general(a, b, (((1,), (1,)), ((), ())), preferred_element_type=F32)


def dot_tn(a, b):
    return lax.dot_general(a, b, (((0,), (0,)), ((), ())), preferred_element_type=F32)


def normalize(values):
    center = jnp.mean(values, axis=-1, keepdims=True)
    shifted = values - center
    inv_spread = lax.rsqrt(jnp.mean(shifted * shifted, axis=-1, keepdims=True) + EPSILON)
    return shifted * inv_spread, inv_spread


def normalize_back(grad_in, normed, inv_spread):
    return inv_spread * (
        grad_in
        - jnp.mean(grad_in, axis=-1, keepdims=True)
        - normed * jnp.mean(grad_in * normed, axis=-1, keepdims=True)
    )


def ranks_column(owner_col, devices):
    rows = owner_col.shape[0]
    match = (owner_col == iota((rows, devices), 1)).astype(F32)
    earlier = (iota((rows, rows), 1) < iota((rows, rows), 0)).astype(BF16)
    before = dot(earlier, match.astype(BF16))
    return jnp.sum(before * match, axis=1, keepdims=True).astype(jnp.int32)


def ranks_row(owner_row, devices):
    rows = owner_row.shape[1]
    match = (owner_row == iota((devices, rows), 0)).astype(F32)
    earlier = (iota((rows, rows), 0) < iota((rows, rows), 1)).astype(BF16)
    before = dot(match.astype(BF16), earlier)
    return jnp.sum(before * match, axis=0, keepdims=True).astype(jnp.int32)


def flat_index():
    return lax.axis_index("dp") * lax.axis_size("cp") + lax.axis_index("cp")


def flat_id(peer):
    size = lax.axis_size("cp")
    return {"dp": lax.div(peer, size), "cp": lax.rem(peer, size)}


def greet(me, count, to_id):
    barrier = pltpu.get_barrier_semaphore()

    @pl.loop(1, count)
    def _(k):
        pl.semaphore_signal(
            barrier, inc=1, device_id=to_id(lax.rem(me + k, count)), device_id_type=MESH
        )

    pl.semaphore_wait(barrier, count - 1)


def fetch_kernel(
    devices, capacity, own_col, own_row, row_col, table_any, scale_ref,
    incoming, got, got_scale,
    request, table, rows_out, scale_out, send_sem, recv_sem, local_sem,
):
    me = flat_index()
    slots = devices * capacity
    load = pltpu.make_async_copy(table_any, table, local_sem.at[0])
    load.start()
    rows = own_col.shape[0]
    rank = ranks_column(own_col[...], devices)
    spread = (rank == iota((rows, LANES), 1)).astype(F32) * (row_col[...] + 1).astype(F32)
    match = (own_row[...] == iota((devices, rows), 0)).astype(F32)
    wanted = (dot_f32(match, spread) + 0.5).astype(jnp.int32)
    for t in range(devices):
        request[t] = wanted[t : t + 1, :]
    greet(me, devices, flat_id)

    def link(kind, src, dst, peer, at_dst, sem):
        return pltpu.make_async_remote_copy(
            src_ref=src.at[peer],
            dst_ref=dst.at[at_dst],
            send_sem=send_sem.at[kind, peer],
            recv_sem=recv_sem.at[kind, sem],
            device_id=flat_id(peer),
            device_id_type=MESH,
        )

    def start(kind, src, dst):
        @pl.loop(1, devices)
        def _(k):
            link(kind, src, dst, lax.rem(me + k, devices), me, me).start()

    def arrive(kind, src, dst):
        @pl.loop(1, devices)
        def _(k):
            peer = lax.rem(me + k, devices)
            link(kind, src, dst, peer, peer, peer).wait_recv()

    def sent(kind, src, dst):
        @pl.loop(1, devices)
        def _(k):
            link(kind, src, dst, lax.rem(me + k, devices), me, me).wait_send()

    start(0, request, incoming)
    incoming[me] = request[me]
    load.wait()
    arrive(0, request, incoming)
    asked = incoming[:, 0, :].astype(F32)
    of_slot = (lax.div(iota((slots, devices), 0), capacity) == iota((slots, devices), 1)).astype(F32)
    lane_of = (lax.rem(iota((slots, LANES), 0), capacity) == iota((slots, LANES), 1)).astype(F32)
    index = (jnp.sum(dot_f32(of_slot, asked) * lane_of, axis=1, keepdims=True) + 0.5).astype(
        jnp.int32
    ) - 1
    total = table.shape[0]
    groups = total // LANES
    high = (lax.shift_right_arithmetic(index, 7) == iota((slots, groups), 1)).astype(F32)
    low = ((index & (LANES - 1)) == iota((slots, LANES), 1)).astype(F32)
    picked = jnp.sum(dot_f32(high, scale_ref[...]) * low, axis=1, keepdims=True)
    to_device = (
        lax.div(iota((devices, slots), 1), capacity) == iota((devices, slots), 0)
    ).astype(F32)
    scales = dot_f32(to_device, picked * lane_of)
    for t in range(devices):
        scale_out[t] = scales[t : t + 1, :]
    start(1, scale_out, got_scale)
    got_scale[me] = scale_out[me]
    one_hot = (index == iota((slots, total), 1)).astype(F32).astype(BF16)
    values = dot(one_hot, table[...])
    for t in range(devices):
        rows_out[t] = values[t * capacity : (t + 1) * capacity, :].astype(BF16)
    start(2, rows_out, got)
    got[me] = rows_out[me]
    arrive(1, scale_out, got_scale)
    arrive(2, rows_out, got)
    sent(0, request, incoming)
    sent(1, scale_out, got_scale)
    sent(2, rows_out, got)


def layer_kernel(
    devices, capacity, cp, lengths, own_col, own_row, got, got_scale, win_any, wout_any, cot_ref,
    layer_out, outgoing,
    win, wout, flat, slots_f32, projected, embedded, normed, gate_s, gm_s,
    snd_k, snd_v, snd_q, all_k, all_v, all_q,
    snd_att, all_att, snd_ga, all_ga, snd_dq, snd_dk, snd_dv, all_dq, all_dk, all_dv,
    weights, slope, dk_sum, dv_sum, gp_s,
    send_sem, recv_sem, local_sem,
):
    me = lax.axis_index("cp")
    rows, width = layer_out.shape
    heads = HEADS
    hd = width // heads
    share = cp // heads
    slots = devices * capacity
    mine = lax.rem(me, share)
    load_in = pltpu.make_async_copy(win_any, win, local_sem.at[0])
    load_out = pltpu.make_async_copy(wout_any, wout, local_sem.at[1])
    load_in.start()
    load_out.start()
    greet(me, cp, lambda peer: {"cp": peer})

    def link(kind, src, dst, peer, send_at, recv_at):
        return pltpu.make_async_remote_copy(
            src_ref=src,
            dst_ref=dst,
            send_sem=send_sem.at[kind, send_at],
            recv_sem=recv_sem.at[kind, recv_at],
            device_id={"cp": peer},
            device_id_type=MESH,
        )

    def spread(kind, src, dst, which):
        @pl.loop(1, cp)
        def _(k):
            peer = lax.rem(me + k, cp)
            link(kind, src.at[which(peer)], dst.at[me], peer, peer, me).start()

        dst[me] = src[which(me)]

    def spread_sent(kind, src, dst, which):
        @pl.loop(1, cp)
        def _(k):
            peer = lax.rem(me + k, cp)
            link(kind, src.at[which(peer)], dst.at[me], peer, peer, me).wait_send()

    def spread_arrive(kind, src, dst):
        @pl.loop(1, cp)
        def _(k):
            peer = lax.rem(me + k, cp)
            link(kind, src.at[0], dst.at[peer], peer, peer, peer).wait_recv()

    def one_out(kind, src, dst, i):
        @pl.when(me != i)
        def _():
            link(kind, src.at[i], dst.at[me], i, i, me).start()

        @pl.when(me == i)
        def _():
            dst[me] = src[i]

    def one_sent(kind, src, dst, i):
        @pl.when(me != i)
        def _():
            link(kind, src.at[i], dst.at[me], i, i, me).wait_send()

    def when_mine(i, body):
        if share == 1:
            body()
        else:
            pl.when(mine == i % share)(body)

    def source(h):
        return h * share + lax.rem(me, share)

    def from_heads(kind, dst, src):
        for h in range(heads):
            peer = source(h)

            @pl.when(peer != me)
            def _():
                link(kind, src.at[0], dst.at[peer], peer, peer, peer).wait_recv()

    owner = own_col[...]
    place = owner * capacity + ranks_column(owner, devices)
    chosen = (place == iota((rows, slots), 1)).astype(F32).astype(BF16)
    for t in range(devices):
        slots_f32[t * capacity : (t + 1) * capacity, :] = got[t].astype(F32)
    lane_of = (ranks_column(owner, devices) == iota((rows, LANES), 1)).astype(F32)
    match = (owner == iota((rows, devices), 1)).astype(F32)
    scale = jnp.sum(dot_f32(match, got_scale[:, 0, :]) * lane_of, axis=1, keepdims=True)
    emb = dot(chosen, slots_f32[...].astype(BF16)) * scale
    embedded[...] = emb
    norm, inv_embed = normalize(emb)
    normed[...] = norm
    norm16 = norm.astype(BF16)
    load_in.wait()
    head_of = lambda peer: lax.div(peer, share)
    for kind, group, snd, full in ((0, 3, snd_k, all_k), (1, 2, snd_q, all_q), (2, 1, snd_v, all_v)):
        part = dot(norm16, win[:, group * width : (group + 1) * width])
        projected[:, group * width : (group + 1) * width] = part
        act = (part * jax.nn.sigmoid(part)).astype(BF16)
        for h in range(heads):
            snd[h] = act[:, h * hd : (h + 1) * hd]
        spread(kind, snd, full, head_of)
    part = dot(norm16, win[:, :width])
    projected[:, :width] = part
    gate_s[...] = (part * jax.nn.sigmoid(part)).astype(BF16).astype(F32)
    load_out.wait()
    gm_s[...] = dot_nt(cot_ref[...], wout[...])
    spread_arrive(0, snd_k, all_k)
    spread_arrive(1, snd_q, all_q)
    spread_arrive(2, snd_v, all_v)

    scaling = hd ** (-0.5)
    documents = lengths.shape[1]
    for i in range(cp):

        def forward(i=i):
            extent = (i + 1) * rows
            keys = all_k[: i + 1].reshape(extent, hd)
            s = dot_nt(all_q[i], keys) * scaling
            pos = i * rows + iota((rows, 1), 0)
            first = jnp.zeros((rows, 1), jnp.int32)
            count = jnp.ones((rows, 1), jnp.int32)
            begin = 0
            for d in range(documents):
                size = lengths[0, d]
                inside = (pos >= begin) & (pos < begin + size)
                first = jnp.where(inside, begin, first)
                count = jnp.where(inside, size, count)
                begin = begin + size
            inverse = 1.0 / count.astype(F32)
            key_pos = iota((rows, extent), 1)
            allowed = (key_pos >= first) & (key_pos <= pos)
            sig = jax.nn.sigmoid(s)
            a = jnp.where(allowed, s * sig * inverse, 0.0).astype(BF16)
            weights[i * rows : (i + 1) * rows, :extent] = a
            slope[i * rows : (i + 1) * rows, :extent] = jnp.where(
                allowed, sig * (1.0 + s * (1.0 - sig)) * (inverse * scaling), 0.0
            )
            snd_att[i] = dot(a, all_v[: i + 1].reshape(extent, hd)).astype(BF16)
            one_out(3, snd_att, all_att, i)

        when_mine(i, forward)

    from_heads(3, all_att, snd_att)
    for h in range(heads):
        flat[:, h * hd : (h + 1) * hd] = all_att[source(h)].astype(F32)
    attn_norm, inv_attn = normalize(flat[...])
    flat[...] = attn_norm
    gm = gm_s[...]
    gate = gate_s[...]
    ga = normalize_back(gm * gate, attn_norm, inv_attn).astype(BF16)
    for h in range(heads):
        snd_ga[h] = ga[:, h * hd : (h + 1) * hd]
    for h in range(heads):
        peer = source(h)

        @pl.when(peer != me)
        def _():
            link(4, snd_ga.at[h], all_ga.at[me], peer, h, me).start()

        @pl.when(peer == me)
        def _():
            all_ga[me] = snd_ga[h]

    def silu_slope(v):
        sig = jax.nn.sigmoid(v)
        return sig * (1.0 + v * (1.0 - sig))

    mixed = (attn_norm * gate).astype(BF16)
    layer_out[...] = (embedded[...] + dot(mixed, wout[...])).astype(BF16)
    grad_u = (gm * attn_norm * silu_slope(projected[:, :width])).astype(BF16)
    gm_s[...] = dot_nt(grad_u, win[:, :width])
    for g in range(1, 4):
        gp_s[:, g * width : (g + 1) * width] = silu_slope(projected[:, g * width : (g + 1) * width])

    dk_sum[...] = jnp.zeros_like(dk_sum)
    dv_sum[...] = jnp.zeros_like(dv_sum)
    for i in reversed(range(cp)):

        def backward(i=i):
            extent = (i + 1) * rows

            @pl.when(me != i)
            def _():
                link(4, snd_ga.at[0], all_ga.at[i], i, 0, i).wait_recv()

            grad = all_ga[i]
            grad_a = dot_nt(grad, all_v[: i + 1].reshape(extent, hd))
            grad_s = (grad_a * slope[i * rows : (i + 1) * rows, :extent]).astype(BF16)
            snd_dq[i] = dot(grad_s, all_k[: i + 1].reshape(extent, hd)).astype(BF16)
            one_out(5, snd_dq, all_dq, i)
            dk_sum[:extent, :] += dot_tn(grad_s, all_q[i])
            dv_sum[:extent, :] += dot_tn(weights[i * rows : (i + 1) * rows, :extent], grad)

        when_mine(i, backward)
        snd_dk[i] = dk_sum[i * rows : (i + 1) * rows, :].astype(BF16)
        one_out(6, snd_dk, all_dk, i)
        snd_dv[i] = dv_sum[i * rows : (i + 1) * rows, :].astype(BF16)
        one_out(7, snd_dv, all_dv, i)

    from_heads(5, all_dq, snd_dq)

    def finish(group, whole, take):
        for h in range(heads):
            at = slice(group * width + h * hd, group * width + (h + 1) * hd)
            whole[:, at] = (take(h) * whole[:, at])

    finish(2, gp_s, lambda h: all_dq[source(h)].astype(F32))
    grad_norm = gm_s[...] + dot_nt(
        gp_s[:, 2 * width : 3 * width].astype(BF16), win[:, 2 * width : 3 * width]
    )
    for kind, group, snd, full in ((6, 3, snd_dk, all_dk), (7, 1, snd_dv, all_dv)):
        spread_arrive(kind, snd, full)

        def summed(h, full=full):
            total = full[h * share].astype(F32)
            for r in range(1, share):
                total = total + full[h * share + r].astype(F32)
            return total

        finish(group, gp_s, summed)
        grad_norm = grad_norm + dot_nt(
            gp_s[:, group * width : (group + 1) * width].astype(BF16),
            win[:, group * width : (group + 1) * width],
        )
    grad_embed = cot_ref[...].astype(F32) + normalize_back(grad_norm, normed[...], inv_embed)
    owner_row = own_row[...]
    place_row = owner_row * capacity + ranks_row(owner_row, devices)
    back = (place_row == iota((slots, rows), 0)).astype(F32).astype(BF16)
    leaving = dot(back, grad_embed.astype(BF16))
    for t in range(devices):
        outgoing[t] = leaving[t * capacity : (t + 1) * capacity, :].astype(BF16)

    for kind, snd, full in ((0, snd_k, all_k), (1, snd_q, all_q), (2, snd_v, all_v)):
        spread_sent(kind, snd, full, head_of)
    for i in range(cp):

        def drained(i=i):
            one_sent(3, snd_att, all_att, i)
            one_sent(5, snd_dq, all_dq, i)

        when_mine(i, drained)
        one_sent(6, snd_dk, all_dk, i)
        one_sent(7, snd_dv, all_dv, i)
    for h in range(heads):
        peer = source(h)

        @pl.when(peer != me)
        def _():
            link(4, snd_ga.at[h], all_ga.at[me], peer, h, me).wait_send()


def return_kernel(devices, src, dst, send_sem, recv_sem, local_sem):
    me = flat_index()
    own = pltpu.make_async_copy(src.at[me], dst.at[me], local_sem)
    own.start()
    greet(me, devices, flat_id)

    def link(peer, at, sem):
        return pltpu.make_async_remote_copy(
            src_ref=src.at[peer],
            dst_ref=dst.at[at],
            send_sem=send_sem.at[peer],
            recv_sem=recv_sem.at[sem],
            device_id=flat_id(peer),
            device_id_type=MESH,
        )

    @pl.loop(1, devices)
    def _(k):
        link(lax.rem(me + k, devices), me, me).start()

    own.wait()

    @pl.loop(1, devices)
    def _(k):
        peer = lax.rem(me + k, devices)
        link(peer, peer, peer).wait_recv()

    @pl.loop(1, devices)
    def _(k):
        link(lax.rem(me + k, devices), me, me).wait_send()


def table_kernel(tile, slots, capacity, lookup, arrived, scale_ref, out):
    base = pl.program_id(0) * tile
    wide = lookup[...] - 1 - base
    one_hot = (wide == iota((tile, slots), 0)).astype(F32).astype(BF16)
    total = dot(one_hot, arrived[...])
    eye = (iota((LANES, LANES), 0) == iota((LANES, LANES), 1)).astype(F32)
    for b in range(tile // LANES):
        column = jnp.sum(eye * scale_ref[b], axis=1, keepdims=True)
        out[b * LANES : (b + 1) * LANES, :] = total[b * LANES : (b + 1) * LANES, :] * column


def per_device(
    table_rows,
    row_scales,
    owners,
    shard_rows,
    history_lengths,
    input_weight,
    output_weight,
    cotangent,
):
    rows = owners.shape[0]
    table_size, width = table_rows.shape
    devices = lax.axis_size(("dp", "cp"))
    cp = lax.axis_size("cp")
    capacity = max(2, 2 * rows // devices)
    slots = devices * capacity
    hd = width // HEADS
    vmem = pl.BlockSpec(memory_space=pltpu.VMEM)
    smem = pl.BlockSpec(memory_space=pltpu.SMEM)
    anywhere = pl.BlockSpec(memory_space=pl.ANY)
    owner_row = owners.reshape(1, rows)
    scale_lines = row_scales.reshape(table_size // LANES, LANES)

    def params(number):
        return pltpu.CompilerParams(
            collective_id=number, has_side_effects=True, vmem_limit_bytes=VMEM_LIMIT
        )

    incoming, got, got_scale = pl.pallas_call(
        functools.partial(fetch_kernel, devices, capacity),
        out_shape=(
            jax.ShapeDtypeStruct((devices, 1, LANES), jnp.int32),
            jax.ShapeDtypeStruct((devices, capacity, width), BF16),
            jax.ShapeDtypeStruct((devices, 1, LANES), F32),
        ),
        in_specs=[vmem, vmem, vmem, anywhere, vmem],
        out_specs=(vmem, vmem, vmem),
        scratch_shapes=[
            pltpu.VMEM((devices, 1, LANES), jnp.int32),
            pltpu.VMEM((table_size, width), BF16),
            pltpu.VMEM((devices, capacity, width), BF16),
            pltpu.VMEM((devices, 1, LANES), F32),
            pltpu.SemaphoreType.DMA((3, devices)),
            pltpu.SemaphoreType.DMA((3, devices)),
            pltpu.SemaphoreType.DMA((1,)),
        ],
        compiler_params=params(0),
    )(owners, owner_row, shard_rows.reshape(rows, 1), table_rows, scale_lines)

    line = cp * rows
    full = lambda: pltpu.VMEM((cp, rows, hd), BF16)
    by_head = lambda: pltpu.VMEM((HEADS, rows, hd), BF16)
    layer_out, outgoing = pl.pallas_call(
        functools.partial(layer_kernel, devices, capacity, cp),
        out_shape=(
            jax.ShapeDtypeStruct((rows, width), BF16),
            jax.ShapeDtypeStruct((devices, capacity, width), BF16),
        ),
        in_specs=[smem, vmem, vmem, vmem, vmem, anywhere, anywhere, vmem],
        out_specs=(vmem, vmem),
        scratch_shapes=[
            pltpu.VMEM(input_weight.shape, BF16),
            pltpu.VMEM(output_weight.shape, BF16),
            pltpu.VMEM((rows, width), F32),
            pltpu.VMEM((slots, width), F32),
            pltpu.VMEM((rows, 4 * width), F32),
            pltpu.VMEM((rows, width), F32),
            pltpu.VMEM((rows, width), F32),
            pltpu.VMEM((rows, width), F32),
            pltpu.VMEM((rows, width), F32),
            by_head(), by_head(), by_head(), full(), full(), full(),
            full(), full(), by_head(), full(), full(), full(), full(), full(), full(), full(),
            pltpu.VMEM((line, line), BF16),
            pltpu.VMEM((line, line), F32),
            pltpu.VMEM((line, hd), F32),
            pltpu.VMEM((line, hd), F32),
            pltpu.VMEM((rows, 4 * width), F32),
            pltpu.SemaphoreType.DMA((8, cp)),
            pltpu.SemaphoreType.DMA((8, cp)),
            pltpu.SemaphoreType.DMA((2,)),
        ],
        compiler_params=params(1),
    )(history_lengths, owners, owner_row, got, got_scale, input_weight, output_weight, cotangent)

    arrived = pl.pallas_call(
        functools.partial(return_kernel, devices),
        out_shape=jax.ShapeDtypeStruct((devices, capacity, width), BF16),
        in_specs=[vmem],
        out_specs=vmem,
        scratch_shapes=[
            pltpu.SemaphoreType.DMA((devices,)),
            pltpu.SemaphoreType.DMA((devices,)),
            pltpu.SemaphoreType.DMA(()),
        ],
        compiler_params=params(2),
    )(outgoing)

    tile = min(256, table_size)
    lookup = incoming[:, 0, :capacity].reshape(1, slots)
    table_grad = pl.pallas_call(
        functools.partial(table_kernel, tile, slots, capacity),
        out_shape=jax.ShapeDtypeStruct((table_size, width), F32),
        grid=(table_size // tile,),
        in_specs=[
            pl.BlockSpec((1, slots), lambda b: (0, 0)),
            pl.BlockSpec((slots, width), lambda b: (0, 0)),
            pl.BlockSpec((tile // LANES, 1, LANES), lambda b: (b, 0, 0)),
        ],
        out_specs=pl.BlockSpec((tile, width), lambda b: (b, 0)),
        compiler_params=pltpu.CompilerParams(vmem_limit_bytes=VMEM_LIMIT // 2),
    )(lookup, arrived.reshape(slots, width), row_scales.reshape(table_size // LANES, 1, LANES))
    return (layer_out, table_grad)


def solution(mesh):
    return jax.shard_map(
        per_device,
        mesh=mesh,
        in_specs=(
            P(("dp", "cp"), None),
            P(("dp", "cp")),
            P(("dp", "cp"), None),
            P(("dp", "cp")),
            P("dp", None),
            P(),
            P(),
            P(("dp", "cp"), None),
        ),
        out_specs=(P(("dp", "cp"), None), P(("dp", "cp"), None)),
        check_vma=False,
    )
```

```python
import functools

import jax
import jax.numpy as jnp
from jax import lax
from jax.experimental import pallas as pl
from jax.experimental.pallas import tpu as pltpu
from jax.sharding import PartitionSpec as P

HEADS = 8
EPSILON = 1e-05
LANES = 128
MESH = pl.DeviceIdType.MESH
EXACT = lax.Precision.HIGHEST
F32 = jnp.float32
BF16 = jnp.bfloat16
VMEM_LIMIT = 60 * 1024 * 1024


def iota(shape, axis):
    return lax.broadcasted_iota(jnp.int32, shape, axis)


def dot_f32(a, b):
    return jnp.dot(a, b, precision=EXACT, preferred_element_type=F32)


def dot(a, b):
    return jnp.dot(a, b, preferred_element_type=F32)


def dot_nt(a, b):
    return lax.dot_general(a, b, (((1,), (1,)), ((), ())), preferred_element_type=F32)


def dot_tn(a, b):
    return lax.dot_general(a, b, (((0,), (0,)), ((), ())), preferred_element_type=F32)


def normalize(values):
    center = jnp.mean(values, axis=-1, keepdims=True)
    shifted = values - center
    inv_spread = lax.rsqrt(jnp.mean(shifted * shifted, axis=-1, keepdims=True) + EPSILON)
    return shifted * inv_spread, inv_spread


def normalize_back(grad_in, normed, inv_spread):
    return inv_spread * (
        grad_in
        - jnp.mean(grad_in, axis=-1, keepdims=True)
        - normed * jnp.mean(grad_in * normed, axis=-1, keepdims=True)
    )


def ranks_column(owner_col, devices):
    rows = owner_col.shape[0]
    match = (owner_col == iota((rows, devices), 1)).astype(F32)
    earlier = (iota((rows, rows), 1) < iota((rows, rows), 0)).astype(BF16)
    before = dot(earlier, match.astype(BF16))
    return jnp.sum(before * match, axis=1, keepdims=True).astype(jnp.int32)


def ranks_row(owner_row, devices):
    rows = owner_row.shape[1]
    match = (owner_row == iota((devices, rows), 0)).astype(F32)
    earlier = (iota((rows, rows), 0) < iota((rows, rows), 1)).astype(BF16)
    before = dot(match.astype(BF16), earlier)
    return jnp.sum(before * match, axis=0, keepdims=True).astype(jnp.int32)


def flat_index():
    return lax.axis_index("dp") * lax.axis_size("cp") + lax.axis_index("cp")


def flat_id(peer):
    size = lax.axis_size("cp")
    return {"dp": lax.div(peer, size), "cp": lax.rem(peer, size)}


def column_of(row):
    size = row.shape[1]
    eye = (iota((size, size), 0) == iota((size, size), 1)).astype(F32)
    return (jnp.sum(eye * row.astype(F32), axis=1, keepdims=True) + 0.5).astype(jnp.int32)


def sigmoid(v):
    return 0.5 * jnp.tanh(0.5 * v) + 0.5


def silu_slope(v):
    sig = sigmoid(v)
    return sig * (1.0 + v * (1.0 - sig))


def layer_kernel(
    devices, capacity, cp, lengths, own_row, row_row, scale_ref, cot_ref, table_any, win_any, wout_any,
    layer_out, lookup, arrived,
    request, incoming, table, rows_out, scale_out, got, got_scale, outgoing,
    win, wout, flat, slots_f32, projected, embedded, normed, gate_s, gm_s,
    snd_k, snd_v, snd_q, all_k, all_v, all_q,
    snd_att, all_att, snd_ga, all_ga, snd_dq, snd_dk, snd_dv, all_dq, all_dk, all_dv,
    weights, slope, dk_sum, dv_sum,
    wide_send, wide_recv, send_sem, recv_sem, local_sem,
):
    whole_me = flat_index()
    me = lax.axis_index("cp")
    rows, width = layer_out.shape
    heads = HEADS
    hd = width // heads
    share = cp // heads
    slots = devices * capacity
    mine = lax.rem(me, share)
    pair = 2 if cp % (2 * share) == 0 else 1
    span = pair * rows
    loads = [
        pltpu.make_async_copy(table_any, table, local_sem.at[0]),
        pltpu.make_async_copy(wout_any, wout, local_sem.at[1]),
        pltpu.make_async_copy(win_any, win, local_sem.at[2]),
    ]
    barrier = pltpu.get_barrier_semaphore()

    @pl.loop(1, devices)
    def _(k):
        pl.semaphore_signal(
            barrier,
            inc=1,
            device_id=flat_id(lax.rem(whole_me + k, devices)),
            device_id_type=MESH,
        )

    for load in loads:
        load.start()

    def wide(kind, src, dst, peer, at, sem):
        return pltpu.make_async_remote_copy(
            src_ref=src.at[peer],
            dst_ref=dst.at[at],
            send_sem=wide_send.at[kind, peer],
            recv_sem=wide_recv.at[kind, sem],
            device_id=flat_id(peer),
            device_id_type=MESH,
        )

    def wide_start(kind, src, dst):
        @pl.loop(1, devices)
        def _(k):
            wide(kind, src, dst, lax.rem(whole_me + k, devices), whole_me, whole_me).start()

        dst[whole_me] = src[whole_me]

    def wide_arrive(kind, src, dst):
        @pl.loop(1, devices)
        def _(k):
            peer = lax.rem(whole_me + k, devices)
            wide(kind, src, dst, peer, peer, peer).wait_recv()

    def wide_sent(kind, src, dst):
        @pl.loop(1, devices)
        def _(k):
            wide(kind, src, dst, lax.rem(whole_me + k, devices), whole_me, whole_me).wait_send()

    def link(kind, src, dst, peer, send_at, recv_at):
        return pltpu.make_async_remote_copy(
            src_ref=src,
            dst_ref=dst,
            send_sem=send_sem.at[kind, send_at],
            recv_sem=recv_sem.at[kind, recv_at],
            device_id={"cp": peer},
            device_id_type=MESH,
        )

    def spread(kind, src, dst, which):
        @pl.loop(1, cp)
        def _(k):
            peer = lax.rem(me + k, cp)
            link(kind, src.at[which(peer)], dst.at[me], peer, peer, me).start()

        dst[me] = src[which(me)]

    def spread_sent(kind, src, dst, which):
        @pl.loop(1, cp)
        def _(k):
            peer = lax.rem(me + k, cp)
            link(kind, src.at[which(peer)], dst.at[me], peer, peer, me).wait_send()

    def spread_arrive(kind, src, dst):
        @pl.loop(1, cp)
        def _(k):
            peer = lax.rem(me + k, cp)
            link(kind, src.at[0], dst.at[peer], peer, peer, peer).wait_recv()

    def one_out(kind, src, dst, i):
        @pl.when(me != i)
        def _():
            link(kind, src.at[i], dst.at[me], i, i, me).start()

        @pl.when(me == i)
        def _():
            dst[me] = src[i]

    def one_sent(kind, src, dst, i):
        @pl.when(me != i)
        def _():
            link(kind, src.at[i], dst.at[me], i, i, me).wait_send()

    def when_mine(i, body):
        if share == 1:
            body()
        else:
            pl.when(mine == i % share)(body)

    def source(h):
        return h * share + lax.rem(lax.div(me, pair), share)

    def from_heads(kind, dst, src):
        for h in range(heads):
            peer = source(h)

            @pl.when(peer != me)
            def _():
                link(kind, src.at[0], dst.at[peer], peer, peer, peer).wait_recv()

    owner_row = own_row[...]
    owner = column_of(owner_row)
    row_index = column_of(row_row[...])
    rank = ranks_column(owner, devices)
    spots = (rank == iota((rows, LANES), 1)).astype(F32)
    named = (owner_row == iota((devices, rows), 0)).astype(F32)
    wanted = (dot_f32(named, spots * (row_index + 1).astype(F32)) + 0.5).astype(jnp.int32)
    for t in range(devices):
        request[t] = wanted[t : t + 1, :]
    pl.semaphore_wait(barrier, devices - 1)
    wide_start(0, request, incoming)
    loads[1].wait()
    gm_s[...] = dot_nt(cot_ref[...], wout[...])
    loads[0].wait()
    wide_arrive(0, request, incoming)

    asked = incoming[:, 0, :].astype(F32)
    of_slot = (lax.div(iota((slots, devices), 0), capacity) == iota((slots, devices), 1)).astype(F32)
    lane_of = (lax.rem(iota((slots, LANES), 0), capacity) == iota((slots, LANES), 1)).astype(F32)
    index = (jnp.sum(dot_f32(of_slot, asked) * lane_of, axis=1, keepdims=True) + 0.5).astype(
        jnp.int32
    ) - 1
    total = table.shape[0]
    one_hot = (index == iota((slots, total), 1)).astype(F32).astype(BF16)
    values = dot(one_hot, table[...])
    for t in range(devices):
        rows_out[t] = values[t * capacity : (t + 1) * capacity, :].astype(BF16)
    wide_start(2, rows_out, got)
    groups = total // LANES
    high = (lax.shift_right_arithmetic(index, 7) == iota((slots, groups), 1)).astype(F32)
    low = ((index & (LANES - 1)) == iota((slots, LANES), 1)).astype(F32)
    picked = jnp.sum(dot_f32(high, scale_ref[...]) * low, axis=1, keepdims=True)
    to_device = (
        lax.div(iota((devices, slots), 1), capacity) == iota((devices, slots), 0)
    ).astype(F32)
    scales = dot_f32(to_device, picked * lane_of)
    for t in range(devices):
        scale_out[t] = scales[t : t + 1, :]
    wide_start(1, scale_out, got_scale)
    lane_col = (lax.rem(iota((LANES, slots), 1), capacity) == iota((LANES, slots), 0)).astype(F32)
    line_up = jnp.sum(dot_f32(asked, lane_col) * to_device, axis=0, keepdims=True)
    lookup[...] = (line_up + 0.5).astype(jnp.int32) - 1
    place = owner * capacity + rank
    chosen = (place == iota((rows, slots), 1)).astype(F32).astype(BF16)
    match = (owner == iota((rows, devices), 1)).astype(F32)
    loads[2].wait()
    wide_arrive(1, scale_out, got_scale)
    scale = jnp.sum(dot_f32(match, got_scale[:, 0, :]) * spots, axis=1, keepdims=True)
    wide_arrive(2, rows_out, got)
    for t in range(devices):
        slots_f32[t * capacity : (t + 1) * capacity, :] = got[t].astype(F32)
    emb = dot(chosen, slots_f32[...].astype(BF16)) * scale
    embedded[...] = emb
    norm, inv_embed = normalize(emb)
    normed[...] = norm
    norm16 = norm.astype(BF16)
    head_of = lambda peer: lax.div(peer, share)
    for kind, group, snd, full in ((0, 3, snd_k, all_k), (1, 2, snd_q, all_q), (2, 1, snd_v, all_v)):
        part = dot(norm16, win[:, group * width : (group + 1) * width])
        projected[:, group * width : (group + 1) * width] = part
        act = (part * sigmoid(part)).astype(BF16)
        for h in range(heads):
            snd[h] = act[:, h * hd : (h + 1) * hd]
        spread(kind, snd, full, head_of)
    part = dot(norm16, win[:, :width])
    gate_s[...] = (part * sigmoid(part)).astype(BF16).astype(F32)
    projected[:, :width] = silu_slope(part)
    for g in range(1, 4):
        at = slice(g * width, (g + 1) * width)
        projected[:, at] = silu_slope(projected[:, at])
    dk_sum[...] = jnp.zeros_like(dk_sum)
    dv_sum[...] = jnp.zeros_like(dv_sum)

    scaling = hd ** (-0.5)
    documents = lengths.shape[1]
    for g in range(cp // pair):
        members = range(g * pair, (g + 1) * pair)
        for i in members:

            @pl.when(me != i)
            def _():
                for kind, snd, full in ((0, snd_k, all_k), (1, snd_q, all_q), (2, snd_v, all_v)):
                    link(kind, snd.at[0], full.at[i], i, i, i).wait_recv()

        def forward(g=g, members=members):
            extent = (g + 1) * span
            here = slice(g * span, (g + 1) * span)
            upto = (g + 1) * pair
            keys = all_k[:upto].reshape(extent, hd)
            s = dot_nt(all_q[g * pair : upto].reshape(span, hd), keys) * scaling
            pos = g * span + iota((span, 1), 0)
            first = jnp.zeros((span, 1), jnp.int32)
            count = jnp.ones((span, 1), jnp.int32)
            begin = 0
            for d in range(documents):
                size = lengths[0, d]
                inside = (pos >= begin) & (pos < begin + size)
                first = jnp.where(inside, begin, first)
                count = jnp.where(inside, size, count)
                begin = begin + size
            inverse = 1.0 / count.astype(F32)
            key_pos = iota((span, extent), 1)
            allowed = (key_pos >= first) & (key_pos <= pos)
            sig = sigmoid(s)
            a = jnp.where(allowed, s * sig * inverse, 0.0).astype(BF16)
            weights[here, :extent] = a
            slope[here, :extent] = jnp.where(
                allowed, sig * (1.0 + s * (1.0 - sig)) * (inverse * scaling), 0.0
            )
            result = dot(a, all_v[:upto].reshape(extent, hd)).astype(BF16)
            for j, i in enumerate(members):
                snd_att[i] = result[j * rows : (j + 1) * rows, :]
                one_out(3, snd_att, all_att, i)

        when_mine(g, forward)

    from_heads(3, all_att, snd_att)
    for h in range(heads):
        flat[:, h * hd : (h + 1) * hd] = all_att[source(h)].astype(F32)
    attn_norm, inv_attn = normalize(flat[...])
    flat[...] = attn_norm
    gm = gm_s[...]
    gate = gate_s[...]
    ga = normalize_back(gm * gate, attn_norm, inv_attn).astype(BF16)
    for h in range(heads):
        snd_ga[h] = ga[:, h * hd : (h + 1) * hd]
    for h in range(heads):
        peer = source(h)

        @pl.when(peer != me)
        def _():
            link(4, snd_ga.at[h], all_ga.at[me], peer, h, me).start()

        @pl.when(peer == me)
        def _():
            all_ga[me] = snd_ga[h]

    mixed = (attn_norm * gate).astype(BF16)
    layer_out[...] = (embedded[...] + dot(mixed, wout[...])).astype(BF16)
    grad_u = (gm * attn_norm * projected[:, :width]).astype(BF16)
    gm_s[...] = dot_nt(grad_u, win[:, :width])
    for g in reversed(range(cp // pair)):
        members = range(g * pair, (g + 1) * pair)

        def backward(g=g, members=members):
            extent = (g + 1) * span
            here = slice(g * span, (g + 1) * span)
            upto = (g + 1) * pair
            for i in members:

                @pl.when(me != i)
                def _():
                    link(4, snd_ga.at[0], all_ga.at[i], i, 0, i).wait_recv()

            grad = all_ga[g * pair : upto].reshape(span, hd)
            grad_a = dot_nt(grad, all_v[:upto].reshape(extent, hd))
            grad_s = (grad_a * slope[here, :extent]).astype(BF16)
            result = dot(grad_s, all_k[:upto].reshape(extent, hd)).astype(BF16)
            for j, i in enumerate(members):
                snd_dq[i] = result[j * rows : (j + 1) * rows, :]
                one_out(5, snd_dq, all_dq, i)
            dk_sum[:extent, :] += dot_tn(grad_s, all_q[g * pair : upto].reshape(span, hd))
            dv_sum[:extent, :] += dot_tn(weights[here, :extent], grad)

        when_mine(g, backward)
        for i in members:
            snd_dk[i] = dk_sum[i * rows : (i + 1) * rows, :].astype(BF16)
            one_out(6, snd_dk, all_dk, i)
            snd_dv[i] = dv_sum[i * rows : (i + 1) * rows, :].astype(BF16)
            one_out(7, snd_dv, all_dv, i)

    from_heads(5, all_dq, snd_dq)

    def finish(group, whole, take):
        for h in range(heads):
            at = slice(group * width + h * hd, group * width + (h + 1) * hd)
            whole[:, at] = (take(h) * whole[:, at])

    finish(2, projected, lambda h: all_dq[source(h)].astype(F32))
    grad_norm = gm_s[...] + dot_nt(
        projected[:, 2 * width : 3 * width].astype(BF16), win[:, 2 * width : 3 * width]
    )
    for kind, group, snd, full in ((6, 3, snd_dk, all_dk), (7, 1, snd_dv, all_dv)):
        spread_arrive(kind, snd, full)

        def summed(h, full=full):
            total = full[h * share].astype(F32)
            for r in range(1, share):
                total = total + full[h * share + r].astype(F32)
            return total

        finish(group, projected, summed)
        grad_norm = grad_norm + dot_nt(
            projected[:, group * width : (group + 1) * width].astype(BF16),
            win[:, group * width : (group + 1) * width],
        )
    grad_embed = cot_ref[...].astype(F32) + normalize_back(grad_norm, normed[...], inv_embed)
    place_row = owner_row * capacity + ranks_row(owner_row, devices)
    back = (place_row == iota((slots, rows), 0)).astype(F32).astype(BF16)
    leaving = dot(back, grad_embed.astype(BF16))
    for t in range(devices):
        outgoing[t] = leaving[t * capacity : (t + 1) * capacity, :].astype(BF16)

    wide_start(3, outgoing, arrived)
    for kind, snd, full in ((0, snd_k, all_k), (1, snd_q, all_q), (2, snd_v, all_v)):
        spread_sent(kind, snd, full, head_of)
    for i in range(cp):

        def drained(i=i):
            one_sent(3, snd_att, all_att, i)
            one_sent(5, snd_dq, all_dq, i)

        when_mine(i // pair, drained)
        one_sent(6, snd_dk, all_dk, i)
        one_sent(7, snd_dv, all_dv, i)
    for h in range(heads):
        peer = source(h)

        @pl.when(peer != me)
        def _():
            link(4, snd_ga.at[h], all_ga.at[me], peer, h, me).wait_send()
    wide_sent(0, request, incoming)
    wide_sent(1, scale_out, got_scale)
    wide_sent(2, rows_out, got)
    wide_arrive(3, outgoing, arrived)
    wide_sent(3, outgoing, arrived)


def table_kernel(tile, slots, lookup, arrived, scale_ref, layer_in, out, layer_out):
    layer_out[...] = layer_in[...]
    base = pl.program_id(0) * tile
    wide = lookup[...] - base
    one_hot = (wide == iota((tile, slots), 0)).astype(F32).astype(BF16)
    total = dot(one_hot, arrived[...])
    eye = (iota((LANES, LANES), 0) == iota((LANES, LANES), 1)).astype(F32)
    for b in range(tile // LANES):
        column = jnp.sum(eye * scale_ref[b], axis=1, keepdims=True)
        out[b * LANES : (b + 1) * LANES, :] = total[b * LANES : (b + 1) * LANES, :] * column


def per_device(
    table_rows,
    row_scales,
    owners,
    shard_rows,
    history_lengths,
    input_weight,
    output_weight,
    cotangent,
):
    rows = owners.shape[0]
    table_size, width = table_rows.shape
    devices = lax.axis_size(("dp", "cp"))
    cp = lax.axis_size("cp")
    capacity = max(2, 2 * rows // devices)
    slots = devices * capacity
    hd = width // HEADS
    vmem = pl.BlockSpec(memory_space=pltpu.VMEM)
    smem = pl.BlockSpec(memory_space=pltpu.SMEM)
    anywhere = pl.BlockSpec(memory_space=pl.ANY)
    owner_row = owners.reshape(1, rows)
    scale_lines = row_scales.reshape(table_size // LANES, LANES)

    line = cp * rows
    slot_rows = lambda: pltpu.VMEM((devices, capacity, width), BF16)
    full = lambda: pltpu.VMEM((cp, rows, hd), BF16)
    by_head = lambda: pltpu.VMEM((HEADS, rows, hd), BF16)
    layer_out, lookup, arrived = pl.pallas_call(
        functools.partial(layer_kernel, devices, capacity, cp),
        out_shape=(
            jax.ShapeDtypeStruct((rows, width), BF16),
            jax.ShapeDtypeStruct((1, slots), jnp.int32),
            jax.ShapeDtypeStruct((devices, capacity, width), BF16),
        ),
        in_specs=[smem, vmem, vmem, vmem, vmem, anywhere, anywhere, anywhere],
        out_specs=(vmem, vmem, vmem),
        scratch_shapes=[
            pltpu.VMEM((devices, 1, LANES), jnp.int32),
            pltpu.VMEM((devices, 1, LANES), jnp.int32),
            pltpu.VMEM((table_size, width), BF16),
            slot_rows(),
            pltpu.VMEM((devices, 1, LANES), F32),
            slot_rows(),
            pltpu.VMEM((devices, 1, LANES), F32),
            slot_rows(),
            pltpu.VMEM(input_weight.shape, BF16),
            pltpu.VMEM(output_weight.shape, BF16),
            pltpu.VMEM((rows, width), F32),
            pltpu.VMEM((slots, width), F32),
            pltpu.VMEM((rows, 4 * width), F32),
            pltpu.VMEM((rows, width), F32),
            pltpu.VMEM((rows, width), F32),
            pltpu.VMEM((rows, width), F32),
            pltpu.VMEM((rows, width), F32),
            by_head(), by_head(), by_head(), full(), full(), full(),
            full(), full(), by_head(), full(), full(), full(), full(), full(), full(), full(),
            pltpu.VMEM((line, line), BF16),
            pltpu.VMEM((line, line), F32),
            pltpu.VMEM((line, hd), F32),
            pltpu.VMEM((line, hd), F32),
            pltpu.SemaphoreType.DMA((4, devices)),
            pltpu.SemaphoreType.DMA((4, devices)),
            pltpu.SemaphoreType.DMA((8, cp)),
            pltpu.SemaphoreType.DMA((8, cp)),
            pltpu.SemaphoreType.DMA((3,)),
        ],
        compiler_params=pltpu.CompilerParams(
            collective_id=0, has_side_effects=True, vmem_limit_bytes=VMEM_LIMIT
        ),
    )(
        history_lengths,
        owner_row,
        shard_rows.reshape(1, rows),
        scale_lines,
        cotangent,
        table_rows,
        input_weight,
        output_weight,
    )

    tile = min(512, table_size)
    table_grad, layer_out = pl.pallas_call(
        functools.partial(table_kernel, tile, slots),
        out_shape=(
            jax.ShapeDtypeStruct((table_size, width), F32),
            jax.ShapeDtypeStruct((rows, width), BF16),
        ),
        grid=(table_size // tile,),
        in_specs=[
            pl.BlockSpec((1, slots), lambda b: (0, 0)),
            pl.BlockSpec((slots, width), lambda b: (0, 0)),
            pl.BlockSpec((tile // LANES, 1, LANES), lambda b: (b, 0, 0)),
            pl.BlockSpec((rows, width), lambda b: (0, 0)),
        ],
        out_specs=(
            pl.BlockSpec((tile, width), lambda b: (b, 0)),
            pl.BlockSpec((rows, width), lambda b: (0, 0)),
        ),
        compiler_params=pltpu.CompilerParams(vmem_limit_bytes=VMEM_LIMIT),
    )(lookup, arrived.reshape(slots, width), row_scales.reshape(table_size // LANES, 1, LANES), layer_out)
    return (layer_out, table_grad)


def solution(mesh):
    return jax.shard_map(
        per_device,
        mesh=mesh,
        in_specs=(
            P(("dp", "cp"), None),
            P(("dp", "cp")),
            P(("dp", "cp"), None),
            P(("dp", "cp")),
            P("dp", None),
            P(),
            P(),
            P(("dp", "cp"), None),
        ),
        out_specs=(P(("dp", "cp"), None), P(("dp", "cp"), None)),
        check_vma=False,
    )
```
